256 devices in a mesh: section: 64 (over z_lo, y, x), tensor: 4 (over z_hi, core).
Axes of the slice: x: 4, y: 4, z: 8 (z_hi: 2, z_lo: 4; z = z_hi * 4 + z_lo), core: 2. Of those that a mesh axis runs over, the one named last changes fastest.
Arguments:
- queries: bfloat16 [8192, 16384], P('section', 'tensor'), may hold values from -108 to 108
- new_keys: bfloat16 [8192, 1024], P('section', 'tensor'), may hold values from -10 to 10
- new_values: bfloat16 [8192, 1024], P('section', 'tensor'), may hold values from -6 to 6
- cache_keys: bfloat16 [65536, 1024], P('section', 'tensor'), may hold values from -6 to 6
- cache_values: bfloat16 [65536, 1024], P('section', 'tensor'), may hold values from -6 to 6
- prior_length: int32 [64], P('section'), may hold values from 1 to 1024, as said below
- placement: int32 [1024, 1], P('section'), may hold values from 0 to 63; in each aligned block of 16 rows (0 to 15, 16 to 31, ...) at most 2 rows name the same one
Outputs:
- handed: bfloat16 [8192, 16384], P(('section', 'tensor'))
- landed: bfloat16 [8192, 8, 2, 1024], P('section', None, None, 'tensor')
The draws below stay inside these ranges and needn't reach their ends.
Inputs may be any that keep to these rules, and one draw needn't show every extreme that they name: `prior_length`: some section has exactly 1024 live cache slots. `placement`: of the 16 blocks of one section, at most 2 go to one destination section, and some destination gets exactly 2.
All inputs are finite; a program needn't handle non-finite values.
Results may differ from the reference program's by a relative error of at most 0.012.
The reference program's roundings to bfloat16 on the way count: a program that leaves them out, or rounds other values in their place, can miss the bound.
Values may be sent and summed in bfloat16 or wider, within the bound.
A program may use at most 64 MiB of HBM per device.

```python
import math
import jax
import jax.numpy as jnp
import numpy as np
from jax import lax

HEAD = 128
HEADS = 128
KV_HEADS = 8
SPAN = 128
CACHE = 1024
BLOCK_TOK = 8
BLOCKS = 16
SLOTS = 2
TOKENS = 8192
CACHE_ROWS = 65536
LANDED = 8192
N_SECTION = 64


def paired(key, lift):
    keys = jax.random.split(key, 6)
    rows = N_SECTION * SPAN
    query = jnp.clip(jax.random.normal(keys[0], (rows, HEADS, HEAD), jnp.float32), -6.0, 6.0)
    keyrow = jnp.clip(jax.random.normal(keys[1], (rows, KV_HEADS, HEAD), jnp.float32), -6.0, 6.0)
    column = jnp.arange(HEAD) % (HEAD // 2)
    slow = (column >= 3 * HEAD // 8).astype(jnp.float32)
    vector = jnp.clip(3.0 * jax.random.normal(keys[2], (rows, KV_HEADS, HEAD), jnp.float32), -9.0, 9.0) * slow
    jitter = 0.2 * jnp.clip(jax.random.normal(keys[3], (rows, KV_HEADS, HEAD), jnp.float32), -3.0, 3.0) * slow
    position = jnp.arange(rows) % SPAN
    picked = jax.random.bernoulli(keys[4], 1.0 / 64.0, (rows,)) & (position > 0) & (lift > 0.0)
    strength = 4.0 * jax.random.randint(keys[5], (rows,), 1, 4).astype(jnp.float32)
    before = jnp.roll(picked, -1)
    vector_next = jnp.roll(vector, -1, axis=0)
    keyrow = jnp.where(picked[:, None, None], vector, jnp.where(before[:, None, None], vector_next + jitter, keyrow))
    aligned = jnp.repeat(vector, HEADS // KV_HEADS, axis=1) * strength[:, None, None]
    query = jnp.where(picked[:, None, None], aligned, query)
    return (query.reshape(rows, HEADS * HEAD), keyrow.reshape(rows, KV_HEADS * HEAD))


def draw_queries(key, part):
    lift = 0.0
    query, keyrow = paired(key, lift)
    return query.astype(jnp.bfloat16)


def draw_new_keys(key, part):
    lift = 0.0
    query, keyrow = paired(key, lift)
    return keyrow.astype(jnp.bfloat16)


def draw_prior_length(key, part):
    key = jax.random.fold_in(key, 7)
    first, second = jax.random.split(key)
    lengths = jax.random.randint(first, (N_SECTION,), 1, CACHE + 1)
    chosen = jax.random.randint(second, (), 0, N_SECTION)
    return lengths.at[chosen].set(CACHE).astype(jnp.int32)


def block_scale(stream_key, extent, pieces, smallest, largest):
    gain = 1.0
    for dim, parts in pieces:
        draws = jax.random.uniform(jax.random.fold_in(jax.random.fold_in(stream_key, 6), dim), (parts,), jnp.float32, smallest / len(pieces), largest / len(pieces))
        gain = gain * jnp.repeat(jnp.exp(draws), extent[dim] // parts).reshape((-1,) + (1,) * (len(extent) - 1 - dim))
    return gain


def routed_block(own_key, own, number, rows, count, top, bound, slope):
    ranking = jax.random.permutation(own_key, count)
    packed, usual = load_shares(count, rows * top, bound, slope, True), load_shares(count, rows * top, bound, slope, False)
    places = jnp.arange(count)

    def named(sizes, rotation):
        used = int((sizes > 0).sum())
        fixed = max(1, used // 4)
        moved = fixed + (places - fixed + rotation * (used - fixed)) % max(1, count - fixed)
        return jnp.zeros((count,), jnp.int32).at[ranking[jnp.where(places < fixed, places, moved)]].set(jnp.asarray(sizes, jnp.int32))

    sizes = jnp.where(number % 4 == 0, named(packed, number // 4), named(usual, number - number // 4 - 1))
    mixed = jax.random.permutation(jax.random.fold_in(own, 3), count)
    source_of, taker = mixed[0:count // 2 * 2:2], mixed[1:count // 2 * 2:2]
    room = jnp.minimum(sizes[source_of] - 1, bound - sizes[taker]) // 2
    room = jnp.where((source_of == ranking[0]) | (taker == ranking[0]) | (sizes[taker] == 0), 0, jnp.maximum(room, 0))
    moved = jax.random.randint(jax.random.fold_in(own, 4), (count // 2,), 0, 1 << 20) % (room + 1)
    sizes = sizes.at[source_of].add(-moved).at[taker].add(moved)
    labels = jnp.searchsorted(jnp.cumsum(sizes), jnp.arange(rows * top), side="right").astype(jnp.int32)
    listing = labels.reshape(top, rows).T
    listing = listing[jax.random.permutation(jax.random.fold_in(own, 1), rows)]
    rotation = jax.random.randint(jax.random.fold_in(own, 2), (rows, 1), 0, top)
    return jnp.take_along_axis(listing, (jnp.arange(top)[None, :] + rotation) % top, axis=1)


def load_shares(amount, total, bound, slope, full):
    weights = [(1 << 20) // math.isqrt(standing ** slope) + 1 for standing in range(1, amount + 1)]
    largest = bound if full else min(bound, max(-(-total // amount), total * weights[0] // sum(weights)))
    least = 1 if total - largest >= amount - 1 else 0
    holding, spare = [largest] + [least] * (amount - 1), total - largest - least * (amount - 1)
    while spare > 0:
        free = [i for i in range(1, amount) if holding[i] < largest] or [i for i in range(1, amount) if holding[i] < bound]
        mass, remaining = sum([weights[i] for i in free]), spare
        for i in free:
            more = min(bound - holding[i], max(1, remaining * weights[i] // mass), spare)
            holding[i] = holding[i] + more
            spare = spare - more
    return np.array(holding)


def noise(key, extent, deviation, most, pieces=(), held_as=jnp.bfloat16):
    result = jax.random.normal(key, extent, jnp.float32) * deviation
    if len(pieces) > 0:
        result = block_scale(key, extent, pieces, -0.22, 0.18) * result
    return jnp.clip(result, min=-most, max=most).astype(held_as)


def setup_inputs(seed: int = 0) -> dict:
    key_list = jax.random.split(jax.random.key(seed), 8)
    queries = draw_queries(jax.random.fold_in(key_list[7], 71), 0)
    new_keys = draw_new_keys(jax.random.fold_in(key_list[7], 71), 0)
    new_values = noise(key_list[2], (TOKENS, KV_HEADS * HEAD), 1.0, 6.0, ((0, 64), (1, 4)))
    cache_keys = noise(key_list[3], (CACHE_ROWS, KV_HEADS * HEAD), 1.0, 6.0, ((0, 64), (1, 4)))
    cache_values = noise(key_list[4], (CACHE_ROWS, KV_HEADS * HEAD), 1.0, 6.0, ((0, 64), (1, 4)))
    prior_length = draw_prior_length(jax.random.fold_in(key_list[7], 71), 0)
    placement_keys = jax.random.split(jax.random.fold_in(key_list[6], 1), (N_SECTION * BLOCKS) // BLOCKS)
    placement_turns = jax.random.permutation(jax.random.fold_in(key_list[6], 3), (N_SECTION * BLOCKS) // BLOCKS)
    placement = jax.vmap(lambda own, number: routed_block(jax.random.fold_in(key_list[6], 2), own, number, BLOCKS, N_SECTION, 1, SLOTS, 2))(placement_keys, placement_turns).reshape((N_SECTION * BLOCKS, 1))
    return dict(queries=queries, new_keys=new_keys, new_values=new_values, cache_keys=cache_keys, cache_values=cache_values, prior_length=prior_length, placement=placement)


def rotate(values, angles):
    half = values.shape[-1] // 2
    cosine = jnp.cos(angles)
    sine = jnp.sin(angles)
    first = values[..., :half]
    second = values[..., half:]
    return jnp.concatenate([first * cosine - second * sine, second * cosine + first * sine], axis=-1)


def angle_table(start, count):
    index = jnp.arange(HEAD // 2, dtype=jnp.float32)
    frequency = jnp.exp(index * (-2.0 / HEAD) * jnp.log(jnp.float32(500000.0)))
    positions = start.astype(jnp.float32) + jnp.arange(count, dtype=jnp.float32)
    return positions[:, None] * frequency[None, :]


def one_section(section_queries, section_keys, section_values, section_cache_keys, section_cache_values, length):
    group = HEADS // KV_HEADS
    angles = angle_table(length, SPAN)
    keys_rotated = rotate(section_keys.astype(jnp.float32).reshape(SPAN, KV_HEADS, HEAD), angles[:, None, :])
    keys_rotated = keys_rotated.astype(jnp.bfloat16).reshape(SPAN, KV_HEADS * HEAD)
    cache_valid = jnp.arange(CACHE) < length
    causal = jnp.arange(SPAN)[None, :] <= jnp.arange(SPAN)[:, None]
    visible = jnp.concatenate([jnp.broadcast_to(cache_valid[None, :], (SPAN, CACHE)), causal], axis=1)
    scale = HEAD ** -0.5

    def per_head(head_index):
        start = (head_index * group * HEAD).astype(jnp.int32)
        query_part = lax.dynamic_slice_in_dim(section_queries, start, group * HEAD, 1)
        query_part = query_part.astype(jnp.float32).reshape(SPAN, group, HEAD)
        query_part = lax.optimization_barrier(rotate(query_part, angles[:, None, :]).astype(jnp.bfloat16))
        column = (head_index * HEAD).astype(jnp.int32)
        keys_all = jnp.concatenate([lax.dynamic_slice_in_dim(section_cache_keys, column, HEAD, 1),
                                    lax.dynamic_slice_in_dim(keys_rotated, column, HEAD, 1)], axis=0)
        values_all = jnp.concatenate([lax.dynamic_slice_in_dim(section_cache_values, column, HEAD, 1),
                                      lax.dynamic_slice_in_dim(section_values, column, HEAD, 1)], axis=0)
        scores = jnp.einsum('cgh,kh->gck', query_part.astype(jnp.float32), keys_all.astype(jnp.float32)) * scale
        scores = jnp.where(visible[None], scores, -1e30)
        top = jnp.max(scores, axis=-1, keepdims=True)
        weights = jnp.where(visible[None], jnp.exp(scores - top), 0.0)
        total = jnp.sum(weights, axis=-1, keepdims=True)
        rounded = lax.optimization_barrier(weights.astype(jnp.bfloat16)).astype(jnp.float32)
        summed = jnp.einsum('gck,kh->gch', rounded, values_all.astype(jnp.float32)) / total
        return jnp.transpose(summed, (1, 0, 2)).reshape(SPAN, group * HEAD).astype(jnp.bfloat16)

    outputs = lax.map(per_head, jnp.arange(KV_HEADS, dtype=jnp.int32))
    attended = jnp.transpose(outputs, (1, 0, 2)).reshape(SPAN, HEADS * HEAD)
    blocks = jnp.stack([keys_rotated, section_values], axis=1).reshape(BLOCKS, BLOCK_TOK, 2, KV_HEADS * HEAD)
    return attended, blocks


def reference(queries, new_keys, new_values, cache_keys, cache_values, prior_length, placement):
    def section_fn(operands):
        return one_section(*operands)

    attended, blocks = lax.map(section_fn, (queries.reshape(N_SECTION, SPAN, HEADS * HEAD),
                                          new_keys.reshape(N_SECTION, SPAN, KV_HEADS * HEAD),
                                          new_values.reshape(N_SECTION, SPAN, KV_HEADS * HEAD),
                                          cache_keys.reshape(N_SECTION, CACHE, KV_HEADS * HEAD),
                                          cache_values.reshape(N_SECTION, CACHE, KV_HEADS * HEAD),
                                          prior_length))
    handed = jnp.roll(attended, 1, axis=0).reshape(TOKENS, HEADS * HEAD)
    target = placement[:, 0].reshape(N_SECTION, BLOCKS).astype(jnp.int32)
    onehot = (target[:, :, None] == jnp.arange(N_SECTION, dtype=jnp.int32)[None, None, :]).astype(jnp.int32)
    earlier = jnp.cumsum(onehot, axis=1) - onehot
    slot = jnp.sum(earlier * onehot, axis=2)
    source = jnp.arange(N_SECTION, dtype=jnp.int32)[:, None]
    index = ((target * N_SECTION + source) * SLOTS + slot).reshape(-1).astype(jnp.int32)
    landed = jnp.zeros((LANDED, BLOCK_TOK, 2, KV_HEADS * HEAD), jnp.bfloat16)
    landed = landed.at[index].set(blocks.reshape(N_SECTION * BLOCKS, BLOCK_TOK, 2, KV_HEADS * HEAD))
    return (handed, landed)
```

```python
import functools

import jax
import jax.numpy as jnp
from jax import lax
from jax.experimental import pallas as pl
from jax.experimental.pallas import tpu as pltpu
from jax.sharding import PartitionSpec as P

MESH = pl.DeviceIdType.MESH
HEAD = 128
ROWS = 128
CACHE = 1024
BLOCK_TOK = 8
PLANE = 16
DEPTH = 4
TENSOR = 4
HEADS = 32
STEP_HEADS = 4
STEPS = HEADS // STEP_HEADS
STEP_COLS = STEP_HEADS * HEAD
KV_WIDTH = 2 * HEAD
ROW_PART = ROWS // TENSOR
MASKED = -1e30


def kernel(
    queries, new_keys, new_values, cache_keys, cache_values, cosine, sine, bias, slots,
    handed, landed,
    attended, held, packed,
    in_send, in_recv, plane_send, plane_recv, own_sem, out_send, out_recv,
):
    section = lax.axis_index("section")
    tensor = lax.axis_index("tensor")
    sections = DEPTH * PLANE
    z, xy = section // PLANE, section % PLANE
    after = lax.rem(section + 1, sections)
    before = lax.rem(section + sections - 1, sections)

    barrier = pltpu.get_barrier_semaphore()

    def greet(device):
        pl.semaphore_signal(barrier, inc=1, device_id=device, device_id_type=MESH)

    for i in range(1, DEPTH):
        greet((lax.rem(z + i, DEPTH) * PLANE + xy, tensor))
    for i in range(TENSOR):
        greet((before, lax.rem(tensor + i, TENSOR)))

    @pl.loop(1, PLANE)
    def _(i):
        greet((z * PLANE + lax.rem(xy + i, PLANE), tensor))

    def rotate(part):
        part = part.astype(jnp.float32)
        turned = pltpu.roll(part, HEAD // 2, 1)
        return (part * cosine[...] + turned * sine[...]).astype(jnp.bfloat16)

    for g in range(2):
        columns = pl.ds(g * HEAD, HEAD)
        held[z, pl.ds(0, ROWS), columns] = rotate(new_keys[:, columns])
    held[z, pl.ds(0, ROWS), pl.ds(KV_WIDTH, KV_WIDTH)] = new_values[...]
    held[z, pl.ds(ROWS, 16), :] = slots[...]

    pl.semaphore_wait(barrier, DEPTH - 1 + TENSOR + PLANE - 1)

    for i in (2, 1, 3):
        pltpu.make_async_remote_copy(
            src_ref=held.at[z], dst_ref=held.at[z], send_sem=in_send, recv_sem=in_recv.at[z],
            device_id=(lax.rem(z + i, DEPTH) * PLANE + xy, tensor), device_id_type=MESH,
        ).start()

    def spread(source):
        row = lax.broadcasted_iota(jnp.int32, (PLANE * 16, ROWS), 0)
        column = lax.broadcasted_iota(jnp.int32, (PLANE * 16, ROWS), 1)
        slot = held[source, pl.ds(ROWS, 16), pl.ds(0, ROWS)].astype(jnp.float32)[0:1, :]
        wanted = (row // BLOCK_TOK + z * PLANE * 2).astype(jnp.float32)
        here = (slot == wanted) & (row % BLOCK_TOK == column % BLOCK_TOK)
        picked = jnp.where(here, 1.0, 0.0).astype(jnp.bfloat16)
        moved = jnp.dot(picked, held[source, pl.ds(0, ROWS), :], preferred_element_type=jnp.float32)
        packed[source] = moved.astype(jnp.bfloat16).reshape(PLANE, 16, 2 * KV_WIDTH)

        @pl.loop(1, PLANE)
        def _(i):
            other = lax.rem(xy + i, PLANE)
            pltpu.make_async_remote_copy(
                src_ref=packed.at[source, other], dst_ref=landed.at[source, xy],
                send_sem=plane_send, recv_sem=plane_recv,
                device_id=(z * PLANE + other, tensor), device_id_type=MESH,
            ).start()
        pltpu.make_async_copy(packed.at[source, xy], landed.at[source, xy], own_sem).start()

    spread(z)

    row = lax.broadcasted_iota(jnp.int32, (ROWS, ROWS), 0)
    column = lax.broadcasted_iota(jnp.int32, (ROWS, ROWS), 1)
    causal = column <= row
    sharp = HEAD ** (-0.5) * 1.4426950408889634

    @pl.loop(0, STEPS)
    def _(step):
        g = step // (STEPS // 2)
        key_columns = pl.ds(pl.multiple_of(g * HEAD, HEAD), HEAD)
        value_columns = pl.ds(pl.multiple_of(KV_WIDTH + g * HEAD, HEAD), HEAD)
        base = step * STEP_COLS
        dims = (((1,), (1,)), ((), ()))
        for h in range(STEP_HEADS):
            columns = pl.ds(pl.multiple_of(base + h * HEAD, HEAD), HEAD)
            query = rotate(queries[:, columns])
            old = lax.dot_general(query, cache_keys[:, key_columns], dims, preferred_element_type=jnp.float32)
            new = lax.dot_general(
                query, held[z, pl.ds(0, ROWS), key_columns], dims, preferred_element_type=jnp.float32
            )
            old = old + bias[...]
            new = jnp.where(causal, new, MASKED)
            top = jnp.maximum(jnp.max(old, axis=1, keepdims=True), jnp.max(new, axis=1, keepdims=True))
            old = jnp.exp2((old - top) * sharp)
            new = jnp.exp2((new - top) * sharp)
            total = jnp.sum(old, axis=1, keepdims=True) + jnp.sum(new, axis=1, keepdims=True)
            summed = jnp.dot(
                old.astype(jnp.bfloat16), cache_values[:, key_columns], preferred_element_type=jnp.float32
            ) + jnp.dot(
                new.astype(jnp.bfloat16), held[z, pl.ds(0, ROWS), value_columns],
                preferred_element_type=jnp.float32,
            )
            attended[:, columns] = (summed / total).astype(jnp.bfloat16)
        for i in (2, 3, 0, 1):
            part = lax.rem(tensor + i, TENSOR)
            pltpu.make_async_remote_copy(
                src_ref=attended.at[
                    pl.ds(pl.multiple_of(part * ROW_PART, ROW_PART), ROW_PART),
                    pl.ds(pl.multiple_of(base, STEP_COLS), STEP_COLS),
                ],
                dst_ref=handed.at[
                    :, pl.ds(pl.multiple_of(tensor * (HEADS * HEAD) + base, STEP_COLS), STEP_COLS)
                ],
                send_sem=out_send, recv_sem=out_recv,
                device_id=(after, part), device_id_type=MESH,
            ).start()

    for i in (1, 3, 2):
        source = lax.rem(z + i, DEPTH)
        pltpu.make_async_copy(held.at[source], held.at[source], in_recv.at[source]).wait()
        spread(source)

    def drain(ref, sem):
        pltpu.make_async_copy(ref, ref, sem).wait()

    drain(held.at[pl.ds(0, DEPTH - 1)], in_send)
    drain(packed.at[:, 0], own_sem)
    drain(packed.at[:, pl.ds(0, PLANE - 1)], plane_send)
    drain(landed.at[:, pl.ds(0, PLANE - 1)], plane_recv)
    drain(attended, out_send)
    drain(handed, out_recv)


def local(queries, new_keys, new_values, cache_keys, cache_values, prior_length, placement):
    length = prior_length[0]
    index = jnp.arange(HEAD // 2, dtype=jnp.float32)
    frequency = jnp.exp(index * (-2.0 / HEAD) * jnp.log(jnp.float32(500000.0)))
    positions = length.astype(jnp.float32) + jnp.arange(ROWS, dtype=jnp.float32)
    angles = positions[:, None] * frequency[None, :]
    cosine, sine = jnp.cos(angles), jnp.sin(angles)
    cosine = jnp.concatenate([cosine, cosine], axis=1)
    sine = jnp.concatenate([-sine, sine], axis=1)
    bias = jnp.where(jnp.arange(CACHE) < length, 0.0, MASKED).astype(jnp.float32)[None, :]
    target = placement[:, 0]
    order = jnp.arange(target.shape[0])
    earlier = (target[None, :] == target[:, None]) & (order[None, :] < order[:, None])
    slot = target * 2 + jnp.sum(earlier.astype(jnp.int32), axis=1)
    lanes = jnp.tile(jnp.repeat(slot, BLOCK_TOK), 2 * KV_WIDTH // ROWS).astype(jnp.bfloat16)
    slots = jnp.broadcast_to(lanes[None, :], (16, 2 * KV_WIDTH))

    vmem = pl.BlockSpec(memory_space=pltpu.VMEM)
    handed, landed = pl.pallas_call(
        kernel,
        out_shape=(
            jax.ShapeDtypeStruct((ROW_PART, TENSOR * HEADS * HEAD), jnp.bfloat16),
            jax.ShapeDtypeStruct((DEPTH, PLANE, 16, 2 * KV_WIDTH), jnp.bfloat16),
        ),
        in_specs=[vmem] * 9,
        out_specs=(vmem, vmem),
        scratch_shapes=[
            pltpu.VMEM((ROWS, HEADS * HEAD), jnp.bfloat16),
            pltpu.VMEM((DEPTH, ROWS + 16, 2 * KV_WIDTH), jnp.bfloat16),
            pltpu.VMEM((DEPTH, PLANE, 16, 2 * KV_WIDTH), jnp.bfloat16),
            pltpu.SemaphoreType.DMA,
            pltpu.SemaphoreType.DMA((DEPTH,)),
            pltpu.SemaphoreType.DMA,
            pltpu.SemaphoreType.DMA,
            pltpu.SemaphoreType.DMA,
            pltpu.SemaphoreType.DMA,
            pltpu.SemaphoreType.DMA,
        ],
        compiler_params=pltpu.CompilerParams(
            collective_id=0, has_side_effects=True, vmem_limit_bytes=40 << 20
        ),
        name="spanned",
    )(queries, new_keys, new_values, cache_keys, cache_values, cosine, sine, bias, slots)
    return handed, landed.reshape(DEPTH * PLANE * 2, BLOCK_TOK, 2, KV_WIDTH)


def solution(mesh):
    placed = (
        P("section", "tensor"),
        P("section", "tensor"),
        P("section", "tensor"),
        P("section", "tensor"),
        P("section", "tensor"),
        P("section"),
        P("section", None),
    )
    return jax.shard_map(
        local,
        mesh=mesh,
        in_specs=placed,
        out_specs=(P(("section", "tensor"), None), P("section", None, None, "tensor")),
        check_vma=False,
    )
```

```python
import functools

import jax
import jax.numpy as jnp
from jax import lax
from jax.experimental import pallas as pl
from jax.experimental.pallas import tpu as pltpu
from jax.sharding import PartitionSpec as P

MESH = pl.DeviceIdType.MESH
HEAD = 128
ROWS = 128
CACHE = 1024
BLOCK_TOK = 8
BLOCKS = ROWS // BLOCK_TOK
PLANE = 16
DEPTH = 4
TENSOR = 4
HEADS = 32
WIDTH = HEADS * HEAD
STEP_HEADS = 4
STEPS = HEADS // STEP_HEADS
STEP_COLS = STEP_HEADS * HEAD
KV_WIDTH = 2 * HEAD
ROW_PART = ROWS // TENSOR
ARRIVAL = 32
AROUND = 2
AROUND_COLS = AROUND * STEP_COLS
MASKED = -1e30
LAG = 3
PASS_AT = 5
ARRIVALS = (2, 4, 6)


def kernel(
    length, placement, queries_hbm, new_keys_hbm, new_values_hbm, cache_keys_hbm, cache_values_hbm,
    handed, landed,
    queries, new_keys, cache_keys, cache_values, cosine, sine, bias, attended, held, packed, passing,
    load_sem, in_send, in_recv, plane_send, plane_recv, own_sem, out_send, out_recv, pass_recv, pass_send,
):
    section = lax.axis_index("section")
    tensor = lax.axis_index("tensor")
    sections = DEPTH * PLANE
    z, xy = section // PLANE, section % PLANE
    core = tensor % 2
    after = lax.rem(section + 1, sections)
    before = lax.rem(section + sections - 1, sections)
    height = tensor // 2 * DEPTH + z
    turning = xy == PLANE - 1

    def at(plane_index, level, core_index):
        level = lax.rem(level, 2 * DEPTH)
        return (lax.rem(level, DEPTH) * PLANE + plane_index, level // DEPTH * 2 + core_index)

    barrier = pltpu.get_barrier_semaphore()

    def greet(device):
        pl.semaphore_signal(barrier, inc=1, device_id=device, device_id_type=MESH)

    for i in range(1, DEPTH):
        greet((lax.rem(z + i, DEPTH) * PLANE + xy, tensor))
    for i in range(TENSOR):
        greet((before, lax.rem(tensor + i, TENSOR)))

    @pl.loop(1, PLANE)
    def _(i):
        greet((z * PLANE + lax.rem(xy + i, PLANE), tensor))

    @pl.when(turning)
    def _():
        greet(at(xy, height + 6, core))

    @pl.when(xy == 0)
    def _():
        for i in range(2):
            greet(at(PLANE - 1, height + 5, i))

    loads = [
        pltpu.make_async_copy(new_keys_hbm, new_keys, load_sem.at[0]),
        pltpu.make_async_copy(new_values_hbm, held.at[z, pl.ds(ROWS, ROWS)], load_sem.at[1]),
        pltpu.make_async_copy(cache_keys_hbm, cache_keys, load_sem.at[2]),
        pltpu.make_async_copy(queries_hbm, queries, load_sem.at[3]),
        pltpu.make_async_copy(cache_values_hbm, cache_values, load_sem.at[4]),
    ]
    for load in loads:
        load.start()

    row = lax.broadcasted_iota(jnp.int32, (ROWS, ROWS), 0)
    column = lax.broadcasted_iota(jnp.int32, (ROWS, ROWS), 1)
    live = length[0]
    index = (column % (HEAD // 2)).astype(jnp.float32)
    frequency = jnp.exp(index[0:8] * (-2.0 / HEAD) * jnp.log(jnp.float32(500000.0)))[0:1]
    angles = (live.astype(jnp.float32) + row.astype(jnp.float32)) * frequency
    cosine[...] = jnp.cos(angles)
    sine[...] = jnp.where(column < HEAD // 2, -1.0, 1.0) * jnp.sin(angles)
    bias[...] = jnp.where(lax.broadcasted_iota(jnp.int32, (1, CACHE), 1) < live, 0.0, MASKED)

    block = lax.broadcasted_iota(jnp.int32, (16, ROWS), 1) // BLOCK_TOK
    target = jnp.zeros((16, ROWS), jnp.int32)
    for b in range(BLOCKS):
        target = jnp.where(block == b, placement[0, b], target)
    slot = target * 2
    for b in range(BLOCKS):
        slot = slot + jnp.where((target == placement[0, b]) & (block > b), 1, 0)
    slot = slot.astype(jnp.float32).astype(jnp.bfloat16)
    held[z, pl.ds(2 * ROWS, 16), :] = jnp.concatenate([slot, slot], axis=1)

    def rotate(part):
        part = part.astype(jnp.float32)
        turned = pltpu.roll(part, HEAD // 2, 1)
        return (part * cosine[...] + turned * sine[...]).astype(jnp.bfloat16)

    loads[0].wait()
    for g in range(2):
        columns = pl.ds(g * HEAD, HEAD)
        held[z, pl.ds(0, ROWS), columns] = rotate(new_keys[:, columns])
    loads[1].wait()

    pl.semaphore_wait(barrier, DEPTH - 1 + TENSOR + PLANE - 1 + jnp.where(turning, 3, 0))

    inner = z % 3 > 0
    nearest = 1 + z % 2
    farthest = jnp.where(z < 2, DEPTH - 1, 0)
    middle = 6 - z - nearest - farthest
    edge = jnp.where(z < 2, 0, DEPTH - 1)

    def gather(source, level):
        pltpu.make_async_remote_copy(
            src_ref=held.at[source], dst_ref=held.at[source], send_sem=in_send, recv_sem=in_recv.at[source],
            device_id=(level * PLANE + xy, tensor), device_id_type=MESH,
        ).start()

    gather(z, nearest)
    gather(z, middle)

    def spread(source):
        tall = PLANE * ARRIVAL
        row = lax.broadcasted_iota(jnp.int32, (tall, ROWS), 0)
        column = lax.broadcasted_iota(jnp.int32, (tall, ROWS), 1)
        slot = held[source, pl.ds(2 * ROWS, 16), pl.ds(0, ROWS)].astype(jnp.float32)[0:1, :]
        wanted = (row // 16 + z * (PLANE * 2)).astype(jnp.float32)
        here = (slot == wanted) & (row % 16 // 2 == column % BLOCK_TOK)
        picked = jnp.concatenate(
            [jnp.where(here & (row % 2 == k), 1.0, 0.0) for k in range(2)], axis=1
        ).astype(jnp.bfloat16)
        moved = jnp.dot(picked, held[source, pl.ds(0, 2 * ROWS), :], preferred_element_type=jnp.float32)
        packed[source] = moved.astype(jnp.bfloat16).reshape(PLANE, ARRIVAL // 2, 2, KV_WIDTH)

        @pl.loop(1, PLANE)
        def _(i):
            other = lax.rem(xy + i, PLANE)
            pltpu.make_async_remote_copy(
                src_ref=packed.at[source, other], dst_ref=landed.at[source, xy],
                send_sem=plane_send, recv_sem=plane_recv,
                device_id=(z * PLANE + other, tensor), device_id_type=MESH,
            ).start()
        pltpu.make_async_copy(packed.at[source, xy], landed.at[source, xy], own_sem).start()

    spread(z)

    for load in loads[2:]:
        load.wait()
    causal = column <= row
    sharp = HEAD ** (-0.5) * 1.4426950408889634
    far = (height + 5) % (2 * DEPTH) // DEPTH * 2

    def hand(part, start, count):
        start = pl.multiple_of(start, STEP_COLS)
        pltpu.make_async_remote_copy(
            src_ref=attended.at[
                pl.ds(pl.multiple_of(part * ROW_PART, ROW_PART), ROW_PART), pl.ds(start, count)
            ],
            dst_ref=handed.at[:, pl.ds(pl.multiple_of(tensor * WIDTH + start, STEP_COLS), count)],
            send_sem=out_send, recv_sem=out_recv,
            device_id=(after, part), device_id_type=MESH,
        ).start()

    crossing = 2 - tensor // 2 * 2
    split = turning & (z < DEPTH - 1)

    def drain(ref, sem):
        pltpu.make_async_copy(ref, ref, sem).wait()

    @pl.loop(0, STEPS)
    def _(step):
        g = step // (STEPS // 2)
        kv_columns = pl.ds(pl.multiple_of(g * HEAD, HEAD), HEAD)
        base = step * STEP_COLS
        dims = (((1,), (1,)), ((), ()))
        for h in range(STEP_HEADS):
            columns = pl.ds(pl.multiple_of(base + h * HEAD, HEAD), HEAD)
            query = rotate(queries[:, columns])
            old = lax.dot_general(query, cache_keys[:, kv_columns], dims, preferred_element_type=jnp.float32)
            new = lax.dot_general(
                query, held[z, pl.ds(0, ROWS), kv_columns], dims, preferred_element_type=jnp.float32
            )
            old = old + bias[...]
            new = jnp.where(causal, new, MASKED)
            top = jnp.maximum(jnp.max(old, axis=1, keepdims=True), jnp.max(new, axis=1, keepdims=True))
            old = jnp.exp2((old - top) * sharp)
            new = jnp.exp2((new - top) * sharp)
            total = jnp.sum(old, axis=1, keepdims=True) + jnp.sum(new, axis=1, keepdims=True)
            summed = jnp.dot(
                old.astype(jnp.bfloat16), cache_values[:, kv_columns], preferred_element_type=jnp.float32
            ) + jnp.dot(
                new.astype(jnp.bfloat16), held[z, pl.ds(ROWS, ROWS), kv_columns],
                preferred_element_type=jnp.float32,
            )
            attended[:, columns] = (summed / total).astype(jnp.bfloat16)

        around = turning & (step < AROUND)

        @pl.when(around)
        def _():
            for i in range(2):
                part = far + i
                pltpu.make_async_remote_copy(
                    src_ref=attended.at[
                        pl.ds(pl.multiple_of(part * ROW_PART, ROW_PART), ROW_PART),
                        pl.ds(pl.multiple_of(base, STEP_COLS), STEP_COLS),
                    ],
                    dst_ref=passing.at[i, :, pl.ds(pl.multiple_of(base, STEP_COLS), STEP_COLS)],
                    send_sem=out_send, recv_sem=pass_recv,
                    device_id=at(xy, height + 2, core), device_id_type=MESH,
                ).start()

        @pl.when(jnp.logical_not(around & (z == DEPTH - 1)))
        def _():
            for i in range(2):
                hand(tensor // 2 * 2 + i, base, STEP_COLS)

        @pl.when((step == LAG) & split)
        def _():
            for i in range(2):
                hand(crossing + i, AROUND_COLS, LAG * STEP_COLS - AROUND_COLS)

        @pl.when((step == LAG) & jnp.logical_not(split))
        def _():
            for i in range(2):
                hand(crossing + i, 0, LAG * STEP_COLS)

        @pl.when(step >= LAG)
        def _():
            for i in range(2):
                hand(crossing + i, base, STEP_COLS)

        @pl.when(turning & (step == PASS_AT))
        def _():
            drain(passing, pass_recv)
            first = lax.rem(height + 6, 2 * DEPTH)
            owner = first // DEPTH * 2 + core
            goal = lax.rem(lax.rem(first, DEPTH) * PLANE + PLANE, sections)
            for i in range(2):
                part = lax.rem(first + 5, 2 * DEPTH) // DEPTH * 2 + i
                pltpu.make_async_remote_copy(
                    src_ref=passing.at[i],
                    dst_ref=handed.at[:, pl.ds(pl.multiple_of(owner * WIDTH, WIDTH), AROUND_COLS)],
                    send_sem=pass_send, recv_sem=out_recv,
                    device_id=(goal, part), device_id_type=MESH,
                ).start()

        sources = (nearest, jnp.where(inner, farthest, middle), jnp.where(inner, middle, farthest))
        for n, when in enumerate(ARRIVALS):
            @pl.when(step == when)
            def _(n=n):
                source = sources[n]
                pltpu.make_async_copy(held.at[source], held.at[source], in_recv.at[source]).wait()
                if n < 2:
                    @pl.when(inner)
                    def _():
                        gather(source, edge)
                spread(source)

    drain(held.at[pl.ds(0, 2)], in_send)

    @pl.when(inner)
    def _():
        drain(held.at[pl.ds(0, 2)], in_send)

    drain(packed.at[:, 0], own_sem)
    drain(packed.at[:, pl.ds(0, PLANE - 1)], plane_send)
    drain(landed.at[:, pl.ds(0, PLANE - 1)], plane_recv)
    drain(attended, out_send)

    @pl.when(turning)
    def _():
        drain(passing, pass_send)

    drain(handed, out_recv)


def local(queries, new_keys, new_values, cache_keys, cache_values, prior_length, placement):
    vmem = pl.BlockSpec(memory_space=pltpu.VMEM)
    smem = pl.BlockSpec(memory_space=pltpu.SMEM)
    hbm = pl.BlockSpec(memory_space=pltpu.HBM)
    half = jnp.bfloat16
    handed, landed = pl.pallas_call(
        kernel,
        out_shape=(
            pltpu.VMEM((ROW_PART, TENSOR * WIDTH), half),
            pltpu.VMEM((DEPTH, PLANE, ARRIVAL // 2, 2, KV_WIDTH), half),
        ),
        in_specs=[smem] * 2 + [hbm] * 5,
        out_specs=(vmem, vmem),
        scratch_shapes=[
            pltpu.VMEM((ROWS, WIDTH), half),
            pltpu.VMEM((ROWS, KV_WIDTH), half),
            pltpu.VMEM((CACHE, KV_WIDTH), half),
            pltpu.VMEM((CACHE, KV_WIDTH), half),
            pltpu.VMEM((ROWS, HEAD), jnp.float32),
            pltpu.VMEM((ROWS, HEAD), jnp.float32),
            pltpu.VMEM((1, CACHE), jnp.float32),
            pltpu.VMEM((ROWS, WIDTH), half),
            pltpu.VMEM((DEPTH, 2 * ROWS + 16, KV_WIDTH), half),
            pltpu.VMEM((DEPTH, PLANE, ARRIVAL // 2, 2, KV_WIDTH), half),
            pltpu.VMEM((2, ROW_PART, AROUND_COLS), half),
            pltpu.SemaphoreType.DMA((5,)),
            pltpu.SemaphoreType.DMA,
            pltpu.SemaphoreType.DMA((DEPTH,)),
        ]
        + [pltpu.SemaphoreType.DMA] * 7,
        compiler_params=pltpu.CompilerParams(
            collective_id=0, has_side_effects=True, vmem_limit_bytes=60 << 20
        ),
        name="spanned",
    )(prior_length, placement.reshape(1, BLOCKS), queries, new_keys, new_values, cache_keys, cache_values)
    return handed, landed.reshape(DEPTH * PLANE * 2, BLOCK_TOK, 2, KV_WIDTH)


def solution(mesh):
    placed = (
        P("section", "tensor"),
        P("section", "tensor"),
        P("section", "tensor"),
        P("section", "tensor"),
        P("section", "tensor"),
        P("section"),
        P("section", None),
    )
    return jax.shard_map(
        local,
        mesh=mesh,
        in_specs=placed,
        out_specs=(P(("section", "tensor"), None), P("section", None, None, "tensor")),
        check_vma=False,
    )
```

```python
import functools

import jax
import jax.numpy as jnp
from jax import lax
from jax.experimental import pallas as pl
from jax.experimental.pallas import tpu as pltpu
from jax.sharding import PartitionSpec as P

MESH = pl.DeviceIdType.MESH
HEAD = 128
ROWS = 128
CACHE = 1024
BLOCK_TOK = 8
BLOCKS = ROWS // BLOCK_TOK
PLANE = 16
DEPTH = 4
TENSOR = 4
HEADS = 32
WIDTH = HEADS * HEAD
STEP_HEADS = 4
STEPS = HEADS // STEP_HEADS
STEP_COLS = STEP_HEADS * HEAD
KV_WIDTH = 2 * HEAD
ROW_PART = ROWS // TENSOR
ARRIVAL = 32
AROUND = 3
MASKED = -1e30
LAG = 3
ARRIVALS = (1, 2, 4)


def kernel(
    length, placement, queries_hbm, new_keys_hbm, new_values_hbm, cache_keys_hbm, cache_values_hbm,
    handed, landed,
    queries, new_keys, cache_keys, cache_values, cosine, sine, bias, attended, held, packed, passing,
    load_sem, in_send, in_recv, plane_send, plane_recv, own_sem, out_send, out_recv, pass_recv, pass_send,
):
    section = lax.axis_index("section")
    tensor = lax.axis_index("tensor")
    sections = DEPTH * PLANE
    z, xy = section // PLANE, section % PLANE
    core = tensor % 2
    after = lax.rem(section + 1, sections)
    before = lax.rem(section + sections - 1, sections)
    height = tensor // 2 * DEPTH + z
    turning = xy == PLANE - 1
    relaying = (xy > 0) & (xy <= 2 * AROUND)

    def at(plane_index, level, core_index):
        level = lax.rem(level, 2 * DEPTH)
        return (lax.rem(level, DEPTH) * PLANE + plane_index, level // DEPTH * 2 + core_index)

    barrier = pltpu.get_barrier_semaphore()

    def greet(device):
        pl.semaphore_signal(barrier, inc=1, device_id=device, device_id_type=MESH)

    for i in range(1, DEPTH):
        greet((lax.rem(z + i, DEPTH) * PLANE + xy, tensor))
    for i in range(TENSOR):
        greet((before, lax.rem(tensor + i, TENSOR)))

    @pl.loop(1, PLANE)
    def _(i):
        greet((z * PLANE + lax.rem(xy + i, PLANE), tensor))

    @pl.when(relaying)
    def _():
        greet(at(PLANE - 1, height, core))

    @pl.when(xy == 0)
    def _():
        for i in range(AROUND):
            for k in range(2):
                greet(at(2 * i + core + 1, height + 3, k))

    loads = [
        pltpu.make_async_copy(new_keys_hbm, new_keys, load_sem.at[0]),
        pltpu.make_async_copy(new_values_hbm, held.at[z, pl.ds(ROWS, ROWS)], load_sem.at[1]),
        pltpu.make_async_copy(cache_keys_hbm, cache_keys, load_sem.at[2]),
        pltpu.make_async_copy(queries_hbm, queries, load_sem.at[3]),
        pltpu.make_async_copy(cache_values_hbm, cache_values, load_sem.at[4]),
    ]
    for load in loads:
        load.start()

    row = lax.broadcasted_iota(jnp.int32, (ROWS, ROWS), 0)
    column = lax.broadcasted_iota(jnp.int32, (ROWS, ROWS), 1)
    live = length[0]
    index = (column % (HEAD // 2)).astype(jnp.float32)
    frequency = jnp.exp(index[0:8] * (-2.0 / HEAD) * jnp.log(jnp.float32(500000.0)))[0:1]
    angles = (live.astype(jnp.float32) + row.astype(jnp.float32)) * frequency
    cosine[...] = jnp.cos(angles)
    sine[...] = jnp.where(column < HEAD // 2, -1.0, 1.0) * jnp.sin(angles)
    bias[...] = jnp.where(lax.broadcasted_iota(jnp.int32, (1, CACHE), 1) < live, 0.0, MASKED)

    block = lax.broadcasted_iota(jnp.int32, (16, ROWS), 1) // BLOCK_TOK
    target = jnp.zeros((16, ROWS), jnp.int32)
    for b in range(BLOCKS):
        target = jnp.where(block == b, placement[0, b], target)
    slot = target * 2
    for b in range(BLOCKS):
        slot = slot + jnp.where((target == placement[0, b]) & (block > b), 1, 0)
    slot = slot.astype(jnp.float32).astype(jnp.bfloat16)
    held[z, pl.ds(2 * ROWS, 16), :] = jnp.concatenate([slot, slot], axis=1)

    def rotate(part):
        part = part.astype(jnp.float32)
        turned = pltpu.roll(part, HEAD // 2, 1)
        return (part * cosine[...] + turned * sine[...]).astype(jnp.bfloat16)

    loads[0].wait()
    for g in range(2):
        columns = pl.ds(g * HEAD, HEAD)
        held[z, pl.ds(0, ROWS), columns] = rotate(new_keys[:, columns])
    loads[1].wait()

    extra = jnp.where(turning, 2 * AROUND, 0) + jnp.where(relaying, 1, 0)
    pl.semaphore_wait(barrier, DEPTH - 1 + TENSOR + PLANE - 1 + extra)

    inner = z % 3 > 0
    nearest = 1 + z % 2
    farthest = jnp.where(z < 2, DEPTH - 1, 0)
    middle = 6 - z - nearest - farthest
    edge = jnp.where(z < 2, 0, DEPTH - 1)

    def gather(source, level):
        pltpu.make_async_remote_copy(
            src_ref=held.at[source], dst_ref=held.at[source], send_sem=in_send, recv_sem=in_recv.at[source],
            device_id=(level * PLANE + xy, tensor), device_id_type=MESH,
        ).start()

    gather(z, nearest)
    gather(z, middle)

    def spread(source):
        tall = PLANE * ARRIVAL
        row = lax.broadcasted_iota(jnp.int32, (tall, ROWS), 0)
        column = lax.broadcasted_iota(jnp.int32, (tall, ROWS), 1)
        slot = held[source, pl.ds(2 * ROWS, 16), pl.ds(0, ROWS)].astype(jnp.float32)[0:1, :]
        wanted = (row // 16 + z * (PLANE * 2)).astype(jnp.float32)
        here = (slot == wanted) & (row % 16 // 2 == column % BLOCK_TOK)
        picked = jnp.concatenate(
            [jnp.where(here & (row % 2 == k), 1.0, 0.0) for k in range(2)], axis=1
        ).astype(jnp.bfloat16)
        moved = jnp.dot(picked, held[source, pl.ds(0, 2 * ROWS), :], preferred_element_type=jnp.float32)
        packed[source] = moved.astype(jnp.bfloat16).reshape(PLANE, ARRIVAL // 2, 2, KV_WIDTH)

        @pl.loop(1, PLANE)
        def _(i):
            other = lax.rem(xy + i, PLANE)
            pltpu.make_async_remote_copy(
                src_ref=packed.at[source, other], dst_ref=landed.at[source, xy],
                send_sem=plane_send, recv_sem=plane_recv,
                device_id=(z * PLANE + other, tensor), device_id_type=MESH,
            ).start()
        pltpu.make_async_copy(packed.at[source, xy], landed.at[source, xy], own_sem).start()

    spread(z)

    for load in loads[2:]:
        load.wait()
    causal = column <= row
    sharp = HEAD ** (-0.5) * 1.4426950408889634
    far = (height + 5) % (2 * DEPTH) // DEPTH * 2

    def hand(part, start, count):
        start = pl.multiple_of(start, STEP_COLS)
        pltpu.make_async_remote_copy(
            src_ref=attended.at[
                pl.ds(pl.multiple_of(part * ROW_PART, ROW_PART), ROW_PART), pl.ds(start, count)
            ],
            dst_ref=handed.at[:, pl.ds(pl.multiple_of(tensor * WIDTH + start, STEP_COLS), count)],
            send_sem=out_send, recv_sem=out_recv,
            device_id=(after, part), device_id_type=MESH,
        ).start()

    crossing = 2 - tensor // 2 * 2
    split = turning & (z < DEPTH - 1)

    def drain(ref, sem):
        pltpu.make_async_copy(ref, ref, sem).wait()

    @pl.loop(0, STEPS)
    def _(step):
        g = step // (STEPS // 2)
        kv_columns = pl.ds(pl.multiple_of(g * HEAD, HEAD), HEAD)
        base = step * STEP_COLS
        dims = (((1,), (1,)), ((), ()))
        for h in range(STEP_HEADS):
            columns = pl.ds(pl.multiple_of(base + h * HEAD, HEAD), HEAD)
            query = rotate(queries[:, columns])
            old = lax.dot_general(query, cache_keys[:, kv_columns], dims, preferred_element_type=jnp.float32)
            new = lax.dot_general(
                query, held[z, pl.ds(0, ROWS), kv_columns], dims, preferred_element_type=jnp.float32
            )
            old = old + bias[...]
            new = jnp.where(causal, new, MASKED)
            top = jnp.maximum(jnp.max(old, axis=1, keepdims=True), jnp.max(new, axis=1, keepdims=True))
            old = jnp.exp2((old - top) * sharp)
            new = jnp.exp2((new - top) * sharp)
            total = jnp.sum(old, axis=1, keepdims=True) + jnp.sum(new, axis=1, keepdims=True)
            summed = jnp.dot(
                old.astype(jnp.bfloat16), cache_values[:, kv_columns], preferred_element_type=jnp.float32
            ) + jnp.dot(
                new.astype(jnp.bfloat16), held[z, pl.ds(ROWS, ROWS), kv_columns],
                preferred_element_type=jnp.float32,
            )
            attended[:, columns] = (summed / total).astype(jnp.bfloat16)

        around = turning & (step < AROUND)

        @pl.when(around)
        def _():
            for i in range(2):
                part = far + i
                pltpu.make_async_remote_copy(
                    src_ref=attended.at[
                        pl.ds(pl.multiple_of(part * ROW_PART, ROW_PART), ROW_PART),
                        pl.ds(pl.multiple_of(base, STEP_COLS), STEP_COLS),
                    ],
                    dst_ref=passing,
                    send_sem=out_send, recv_sem=pass_recv,
                    device_id=at(2 * step + i + 1, height, core), device_id_type=MESH,
                ).start()

        @pl.when(jnp.logical_not(around & (z == DEPTH - 1)))
        def _():
            for i in range(2):
                hand(tensor // 2 * 2 + i, base, STEP_COLS)

        @pl.when((step == LAG) & jnp.logical_not(split))
        def _():
            for i in range(2):
                hand(crossing + i, 0, LAG * STEP_COLS)

        @pl.when(step >= jnp.where(split, AROUND, LAG))
        def _():
            for i in range(2):
                hand(crossing + i, base, STEP_COLS)

        sources = (nearest, jnp.where(inner, farthest, middle), jnp.where(inner, middle, farthest))
        for n, when in enumerate(ARRIVALS):
            @pl.when(step == when)
            def _(n=n):
                source = sources[n]
                pltpu.make_async_copy(held.at[source], held.at[source], in_recv.at[source]).wait()
                if n < 2:
                    @pl.when(inner)
                    def _():
                        gather(source, edge)
                spread(source)

    @pl.when(relaying)
    def _():
        drain(passing, pass_recv)
        start = tensor * WIDTH + (xy - 1) // 2 * STEP_COLS
        pltpu.make_async_remote_copy(
            src_ref=passing,
            dst_ref=handed.at[:, pl.ds(pl.multiple_of(start, STEP_COLS), STEP_COLS)],
            send_sem=pass_send, recv_sem=out_recv,
            device_id=at(0, height + 5, lax.rem(xy + 1, 2)), device_id_type=MESH,
        ).start()

    drain(held.at[pl.ds(0, 2)], in_send)

    @pl.when(inner)
    def _():
        drain(held.at[pl.ds(0, 2)], in_send)

    drain(packed.at[:, 0], own_sem)
    drain(packed.at[:, pl.ds(0, PLANE - 1)], plane_send)
    drain(landed.at[:, pl.ds(0, PLANE - 1)], plane_recv)
    drain(attended, out_send)

    @pl.when(relaying)
    def _():
        drain(passing, pass_send)

    drain(handed, out_recv)


def settle(handed, landed, handed_out, landed_out, sem):
    copies = [
        pltpu.make_async_copy(landed, landed_out, sem.at[0]),
        pltpu.make_async_copy(handed, handed_out, sem.at[1]),
    ]
    for copy in copies:
        copy.start()
    for copy in copies:
        copy.wait()


def local(queries, new_keys, new_values, cache_keys, cache_values, prior_length, placement):
    vmem = pl.BlockSpec(memory_space=pltpu.VMEM)
    smem = pl.BlockSpec(memory_space=pltpu.SMEM)
    hbm = pl.BlockSpec(memory_space=pltpu.HBM)
    half = jnp.bfloat16
    handed, landed = pl.pallas_call(
        kernel,
        out_shape=(
            pltpu.VMEM((ROW_PART, TENSOR * WIDTH), half),
            pltpu.VMEM((DEPTH, PLANE, ARRIVAL // 2, 2, KV_WIDTH), half),
        ),
        in_specs=[smem] * 2 + [hbm] * 5,
        out_specs=(vmem, vmem),
        scratch_shapes=[
            pltpu.VMEM((ROWS, WIDTH), half),
            pltpu.VMEM((ROWS, KV_WIDTH), half),
            pltpu.VMEM((CACHE, KV_WIDTH), half),
            pltpu.VMEM((CACHE, KV_WIDTH), half),
            pltpu.VMEM((ROWS, HEAD), jnp.float32),
            pltpu.VMEM((ROWS, HEAD), jnp.float32),
            pltpu.VMEM((1, CACHE), jnp.float32),
            pltpu.VMEM((ROWS, WIDTH), half),
            pltpu.VMEM((DEPTH, 2 * ROWS + 16, KV_WIDTH), half),
            pltpu.VMEM((DEPTH, PLANE, ARRIVAL // 2, 2, KV_WIDTH), half),
            pltpu.VMEM((ROW_PART, STEP_COLS), half),
            pltpu.SemaphoreType.DMA((5,)),
            pltpu.SemaphoreType.DMA,
            pltpu.SemaphoreType.DMA((DEPTH,)),
        ]
        + [pltpu.SemaphoreType.DMA] * 7,
        compiler_params=pltpu.CompilerParams(
            collective_id=0, has_side_effects=True, vmem_limit_bytes=60 << 20
        ),
        name="spanned",
    )(prior_length, placement.reshape(1, BLOCKS), queries, new_keys, new_values, cache_keys, cache_values)
    landed = landed.reshape(DEPTH * PLANE * 2, BLOCK_TOK, 2, KV_WIDTH)
    return pl.pallas_call(
        settle,
        out_shape=(
            jax.ShapeDtypeStruct(handed.shape, half),
            jax.ShapeDtypeStruct(landed.shape, half),
        ),
        in_specs=[vmem] * 2,
        out_specs=(hbm, hbm),
        scratch_shapes=[pltpu.SemaphoreType.DMA((2,))],
        compiler_params=pltpu.CompilerParams(vmem_limit_bytes=8 << 20),
        name="settle",
    )(handed, landed)


def solution(mesh):
    placed = (
        P("section", "tensor"),
        P("section", "tensor"),
        P("section", "tensor"),
        P("section", "tensor"),
        P("section", "tensor"),
        P("section"),
        P("section", None),
    )
    return jax.shard_map(
        local,
        mesh=mesh,
        in_specs=placed,
        out_specs=(P(("section", "tensor"), None), P("section", None, None, "tensor")),
        check_vma=False,
    )
```

```python
import jax
import jax.numpy as jnp
from jax import lax
from jax.experimental import pallas as pl
from jax.experimental.pallas import tpu as pltpu
from jax.sharding import PartitionSpec as P

MESH = pl.DeviceIdType.MESH
HEAD = 128
ROWS = 128
CACHE = 1024
BLOCK_TOK = 8
BLOCKS = ROWS // BLOCK_TOK
PLANE = 16
DEPTH = 4
TENSOR = 4
HEADS = 32
WIDTH = HEADS * HEAD
STEP_HEADS = 4
STEPS = HEADS // STEP_HEADS
STEP_COLS = STEP_HEADS * HEAD
KV_WIDTH = 2 * HEAD
ROW_PART = ROWS // TENSOR
ARRIVAL = 32
AROUND = 3
MASKED = -1e30
LAG = 5
ARRIVALS = (1, 3, 5)


def kernel(
    length, placement_hbm, queries_hbm, new_keys_hbm, new_values_hbm, cache_keys_hbm, cache_values_hbm,
    handed, landed,
    placement, queries, new_keys, cache_keys, cache_values, cosine, sine, bias, attended, held, packed, passing,
    load_sem, in_send, in_recv, plane_send, plane_recv, own_sem, out_send, out_recv, pass_recv, pass_send,
):
    section = lax.axis_index("section")
    tensor = lax.axis_index("tensor")
    sections = DEPTH * PLANE
    z, xy = section // PLANE, section % PLANE
    core = tensor % 2
    after = lax.rem(section + 1, sections)
    before = lax.rem(section + sections - 1, sections)
    height = tensor // 2 * DEPTH + z
    turning = xy == PLANE - 1
    relaying = (xy > 0) & (xy <= 2 * AROUND)

    def at(plane_index, level, core_index):
        level = lax.rem(level, 2 * DEPTH)
        return (lax.rem(level, DEPTH) * PLANE + plane_index, level // DEPTH * 2 + core_index)

    barrier = pltpu.get_barrier_semaphore()

    def greet(device):
        pl.semaphore_signal(barrier, inc=1, device_id=device, device_id_type=MESH)

    for i in range(1, DEPTH):
        greet((lax.rem(z + i, DEPTH) * PLANE + xy, tensor))
    for i in range(TENSOR):
        greet((before, lax.rem(tensor + i, TENSOR)))

    @pl.loop(1, PLANE)
    def _(i):
        greet((z * PLANE + lax.rem(xy + i, PLANE), tensor))

    @pl.when(relaying)
    def _():
        greet(at(PLANE - 1, height, core))

    @pl.when(xy == 0)
    def _():
        for i in range(AROUND):
            for k in range(2):
                greet(at(2 * i + core + 1, height + 3, k))

    loads = [
        pltpu.make_async_copy(new_keys_hbm, new_keys, load_sem.at[0]),
        pltpu.make_async_copy(new_values_hbm, held.at[z, pl.ds(ROWS, ROWS)], load_sem.at[1]),
        pltpu.make_async_copy(cache_keys_hbm, cache_keys, load_sem.at[2]),
        pltpu.make_async_copy(queries_hbm, queries, load_sem.at[3]),
        pltpu.make_async_copy(cache_values_hbm, cache_values, load_sem.at[4]),
        pltpu.make_async_copy(placement_hbm, placement, load_sem.at[5]),
    ]
    for load in loads[5:] + loads[:5]:
        load.start()
    for load in loads[5:]:
        load.wait()

    row = lax.broadcasted_iota(jnp.int32, (ROWS, ROWS), 0)
    column = lax.broadcasted_iota(jnp.int32, (ROWS, ROWS), 1)
    live = length[0]
    index = (column % (HEAD // 2)).astype(jnp.float32)
    frequency = jnp.exp(index[0:8] * (-2.0 / HEAD) * jnp.log(jnp.float32(500000.0)))[0:1]
    angles = (live.astype(jnp.float32) + row.astype(jnp.float32)) * frequency
    cosine[...] = jnp.cos(angles)
    sine[...] = jnp.where(column < HEAD // 2, -1.0, 1.0) * jnp.sin(angles)
    bias[...] = jnp.where(lax.broadcasted_iota(jnp.int32, (1, CACHE), 1) < live, 0.0, MASKED)

    block = lax.broadcasted_iota(jnp.int32, (16, ROWS), 1) // BLOCK_TOK
    target = jnp.zeros((16, ROWS), jnp.int32)
    for b in range(BLOCKS):
        target = jnp.where(block == b, placement[0, b], target)
    slot = target * 2
    for b in range(BLOCKS):
        slot = slot + jnp.where((target == placement[0, b]) & (block > b), 1, 0)
    slot = slot.astype(jnp.float32).astype(jnp.bfloat16)
    held[z, pl.ds(2 * ROWS, 16), :] = jnp.concatenate([slot, slot], axis=1)

    def rotate(part):
        part = part.astype(jnp.float32)
        turned = pltpu.roll(part, HEAD // 2, 1)
        return (part * cosine[...] + turned * sine[...]).astype(jnp.bfloat16)

    loads[0].wait()
    for g in range(2):
        columns = pl.ds(g * HEAD, HEAD)
        held[z, pl.ds(0, ROWS), columns] = rotate(new_keys[:, columns])
    loads[1].wait()

    extra = jnp.where(turning, 2 * AROUND, 0) + jnp.where(relaying, 1, 0)
    pl.semaphore_wait(barrier, DEPTH - 1 + TENSOR + PLANE - 1 + extra)

    inner = z % 3 > 0
    nearest = 1 + z % 2
    farthest = jnp.where(z < 2, DEPTH - 1, 0)
    middle = 6 - z - nearest - farthest
    edge = jnp.where(z < 2, 0, DEPTH - 1)

    def gather(source, level):
        pltpu.make_async_remote_copy(
            src_ref=held.at[source], dst_ref=held.at[source], send_sem=in_send, recv_sem=in_recv.at[source],
            device_id=(level * PLANE + xy, tensor), device_id_type=MESH,
        ).start()

    gather(z, nearest)
    gather(z, middle)

    def spread(source):
        tall = PLANE * ARRIVAL
        row = lax.broadcasted_iota(jnp.int32, (tall, ROWS), 0)
        column = lax.broadcasted_iota(jnp.int32, (tall, ROWS), 1)
        slot = held[source, pl.ds(2 * ROWS, 16), pl.ds(0, ROWS)].astype(jnp.float32)[0:1, :]
        wanted = (row // 16 + z * (PLANE * 2)).astype(jnp.float32)
        here = (slot == wanted) & (row % 16 // 2 == column % BLOCK_TOK)
        picked = jnp.concatenate(
            [jnp.where(here & (row % 2 == k), 1.0, 0.0) for k in range(2)], axis=1
        ).astype(jnp.bfloat16)
        moved = jnp.dot(picked, held[source, pl.ds(0, 2 * ROWS), :], preferred_element_type=jnp.float32)
        packed[source] = moved.astype(jnp.bfloat16).reshape(PLANE, ARRIVAL // 2, 2, KV_WIDTH)

        @pl.loop(1, PLANE)
        def _(i):
            other = lax.rem(xy + i, PLANE)
            pltpu.make_async_remote_copy(
                src_ref=packed.at[source, other], dst_ref=landed.at[source, xy],
                send_sem=plane_send, recv_sem=plane_recv,
                device_id=(z * PLANE + other, tensor), device_id_type=MESH,
            ).start()
        pltpu.make_async_copy(packed.at[source, xy], landed.at[source, xy], own_sem).start()

    spread(z)

    for load in loads[2:5]:
        load.wait()
    causal = column <= row
    sharp = HEAD ** (-0.5) * 1.4426950408889634
    far = (height + 5) % (2 * DEPTH) // DEPTH * 2

    def hand(part, start, count):
        start = pl.multiple_of(start, STEP_COLS)
        pltpu.make_async_remote_copy(
            src_ref=attended.at[
                pl.ds(pl.multiple_of(part * ROW_PART, ROW_PART), ROW_PART), pl.ds(start, count)
            ],
            dst_ref=handed.at[:, pl.ds(pl.multiple_of(tensor * WIDTH + start, STEP_COLS), count)],
            send_sem=out_send, recv_sem=out_recv,
            device_id=(after, part), device_id_type=MESH,
        ).start()

    crossing = 2 - tensor // 2 * 2
    split = turning & (z < DEPTH - 1)

    def drain(ref, sem):
        pltpu.make_async_copy(ref, ref, sem).wait()

    @pl.loop(0, STEPS)
    def _(step):
        g = step // (STEPS // 2)
        kv_columns = pl.ds(pl.multiple_of(g * HEAD, HEAD), HEAD)
        base = step * STEP_COLS
        dims = (((1,), (1,)), ((), ()))
        rows_of = []
        for h in range(STEP_HEADS):
            columns = pl.ds(pl.multiple_of(base + h * HEAD, HEAD), HEAD)
            query = rotate(queries[:, columns])
            old = lax.dot_general(query, cache_keys[:, kv_columns], dims, preferred_element_type=jnp.float32)
            new = lax.dot_general(
                query, held[z, pl.ds(0, ROWS), kv_columns], dims, preferred_element_type=jnp.float32
            )
            rows_of.append((columns, old + bias[...], jnp.where(causal, new, MASKED)))
        for columns, old, new in rows_of:
            top = jnp.maximum(jnp.max(old, axis=1, keepdims=True), jnp.max(new, axis=1, keepdims=True))
            old = jnp.exp2((old - top) * sharp)
            new = jnp.exp2((new - top) * sharp)
            total = jnp.sum(old, axis=1, keepdims=True) + jnp.sum(new, axis=1, keepdims=True)
            summed = jnp.dot(
                old.astype(jnp.bfloat16), cache_values[:, kv_columns], preferred_element_type=jnp.float32
            ) + jnp.dot(
                new.astype(jnp.bfloat16), held[z, pl.ds(ROWS, ROWS), kv_columns],
                preferred_element_type=jnp.float32,
            )
            attended[:, columns] = (summed / total).astype(jnp.bfloat16)

        around = turning & (step < AROUND)

        @pl.when(around)
        def _():
            for i in range(2):
                part = far + i
                pltpu.make_async_remote_copy(
                    src_ref=attended.at[
                        pl.ds(pl.multiple_of(part * ROW_PART, ROW_PART), ROW_PART),
                        pl.ds(pl.multiple_of(base, STEP_COLS), STEP_COLS),
                    ],
                    dst_ref=passing,
                    send_sem=out_send, recv_sem=pass_recv,
                    device_id=at(2 * step + i + 1, height, core), device_id_type=MESH,
                ).start()

        @pl.when(jnp.logical_not(around & (z == DEPTH - 1)))
        def _():
            for i in range(2):
                hand(tensor // 2 * 2 + i, base, STEP_COLS)

        @pl.when((step == LAG) & jnp.logical_not(split))
        def _():
            for i in range(2):
                hand(crossing + i, 0, LAG * STEP_COLS)

        @pl.when(step >= jnp.where(split, AROUND, LAG))
        def _():
            for i in range(2):
                hand(crossing + i, base, STEP_COLS)

        sources = (nearest, jnp.where(inner, farthest, middle), jnp.where(inner, middle, farthest))
        for n, when in enumerate(ARRIVALS):
            @pl.when(step == when)
            def _(n=n):
                source = sources[n]
                pltpu.make_async_copy(held.at[source], held.at[source], in_recv.at[source]).wait()
                if n < 2:
                    @pl.when(inner)
                    def _():
                        gather(source, edge)
                spread(source)

    @pl.when(relaying)
    def _():
        drain(passing, pass_recv)
        start = tensor * WIDTH + (xy - 1) // 2 * STEP_COLS
        pltpu.make_async_remote_copy(
            src_ref=passing,
            dst_ref=handed.at[:, pl.ds(pl.multiple_of(start, STEP_COLS), STEP_COLS)],
            send_sem=pass_send, recv_sem=out_recv,
            device_id=at(0, height + 5, lax.rem(xy + 1, 2)), device_id_type=MESH,
        ).start()

    drain(held.at[pl.ds(0, 2)], in_send)

    @pl.when(inner)
    def _():
        drain(held.at[pl.ds(0, 2)], in_send)

    drain(packed.at[:, 0], own_sem)
    drain(packed.at[:, pl.ds(0, PLANE - 1)], plane_send)
    drain(landed.at[:, pl.ds(0, PLANE - 1)], plane_recv)
    drain(attended, out_send)

    @pl.when(relaying)
    def _():
        drain(passing, pass_send)

    drain(handed, out_recv)


def settle(handed, landed, handed_out, landed_out, sem):
    copies = [
        pltpu.make_async_copy(landed, landed_out, sem.at[0]),
        pltpu.make_async_copy(handed, handed_out, sem.at[1]),
    ]
    for copy in copies:
        copy.start()
    for copy in copies:
        copy.wait()


def local(queries, new_keys, new_values, cache_keys, cache_values, prior_length, placement):
    vmem = pl.BlockSpec(memory_space=pltpu.VMEM)
    smem = pl.BlockSpec(memory_space=pltpu.SMEM)
    hbm = pl.BlockSpec(memory_space=pltpu.HBM)
    half = jnp.bfloat16
    handed, landed = pl.pallas_call(
        kernel,
        out_shape=(
            pltpu.VMEM((ROW_PART, TENSOR * WIDTH), half),
            pltpu.VMEM((DEPTH, PLANE, ARRIVAL // 2, 2, KV_WIDTH), half),
        ),
        in_specs=[smem] + [hbm] * 6,
        out_specs=(vmem, vmem),
        scratch_shapes=[
            pltpu.SMEM((1, BLOCKS), jnp.int32),
            pltpu.VMEM((ROWS, WIDTH), half),
            pltpu.VMEM((ROWS, KV_WIDTH), half),
            pltpu.VMEM((CACHE, KV_WIDTH), half),
            pltpu.VMEM((CACHE, KV_WIDTH), half),
            pltpu.VMEM((ROWS, HEAD), jnp.float32),
            pltpu.VMEM((ROWS, HEAD), jnp.float32),
            pltpu.VMEM((1, CACHE), jnp.float32),
            pltpu.VMEM((ROWS, WIDTH), half),
            pltpu.VMEM((DEPTH, 2 * ROWS + 16, KV_WIDTH), half),
            pltpu.VMEM((DEPTH, PLANE, ARRIVAL // 2, 2, KV_WIDTH), half),
            pltpu.VMEM((ROW_PART, STEP_COLS), half),
            pltpu.SemaphoreType.DMA((6,)),
            pltpu.SemaphoreType.DMA,
            pltpu.SemaphoreType.DMA((DEPTH,)),
        ]
        + [pltpu.SemaphoreType.DMA] * 7,
        compiler_params=pltpu.CompilerParams(
            collective_id=0, has_side_effects=True, vmem_limit_bytes=60 << 20
        ),
        name="spanned",
    )(prior_length, placement.reshape(1, BLOCKS), queries, new_keys, new_values, cache_keys, cache_values)
    landed = landed.reshape(DEPTH * PLANE * 2, BLOCK_TOK, 2, KV_WIDTH)
    return pl.pallas_call(
        settle,
        out_shape=(
            jax.ShapeDtypeStruct(handed.shape, half),
            jax.ShapeDtypeStruct(landed.shape, half),
        ),
        in_specs=[vmem] * 2,
        out_specs=(hbm, hbm),
        scratch_shapes=[pltpu.SemaphoreType.DMA((2,))],
        compiler_params=pltpu.CompilerParams(vmem_limit_bytes=8 << 20),
        name="settle",
    )(handed, landed)


def solution(mesh):
    placed = (
        P("section", "tensor"),
        P("section", "tensor"),
        P("section", "tensor"),
        P("section", "tensor"),
        P("section", "tensor"),
        P("section"),
        P("section", None),
    )
    return jax.shard_map(
        local,
        mesh=mesh,
        in_specs=placed,
        out_specs=(P(("section", "tensor"), None), P("section", None, None, "tensor")),
        check_vma=False,
    )
```
